32 devices in a mesh: groups: 2 (over y), dom: 16 (over z, x, core).
Axes of the slice: x: 2, y: 2, z: 4, core: 2. Of those that a mesh axis runs over, the one named last changes fastest.
Arguments:
- cartesian_places: float32 [3, 8192], P(None, ('groups', 'dom')), parts along dimension 1, may hold values from 0 to 16, as said below
- node_descriptors: bfloat16 [8192, 128], P(('groups', 'dom')), parts along dimension 0, may hold values from -12 to 12
- padded_partner_list: int32 [8192, 64], P(('groups', 'dom')), parts along dimension 0, may hold values from 0 to 383, as said below
- active_partner_number: int32 [8192], P(('groups', 'dom')), parts along dimension 0, may hold values from 32 to 64, as said below
- exported_site_indices: int32 [4096], P(('groups', 'dom')), parts along dimension 0, may hold values from 0 to 255, as said below
- fourier_modes: int32 [3, 12288], replicated, may hold values from -8 to 48, as said below
- hidden_pole_projection: bfloat16 [128, 16], replicated, may hold values from -0.5 to 0.5
- distance_mlp_first_matrix: bfloat16 [16, 128], replicated, may hold values from -1.5 to 1.5
- distance_mlp_second_matrix: bfloat16 [128, 128], replicated, may hold values from -0.5 to 0.5
- distance_mlp_final_matrix: bfloat16 [128, 128], replicated, may hold values from -0.5 to 0.5
- energy_projection: float32 [128], replicated, may hold values from -4 to 4
Outputs:
- forces: float32 [3, 8192], P(None, ('groups', 'dom')), parts along dimension 1
- feature_grad: bfloat16 [8192, 128], P(('groups', 'dom')), parts along dimension 0
The draws below stay inside these ranges and needn't reach their ends.
There are 2 independent parts, one for each index of `groups`. The reference program is written for one: setup_inputs(seed, part) draws one part's arguments, and reference() takes and returns one part's arrays. A program takes and returns all parts, laid end to end along the dimension named above; an argument that names none is the same for every part. Nothing has to cross between parts.
Inputs may be any that keep to these rules, and one draw needn't show every extreme that they name: `cartesian_places`: atom a has x between a // 256 and a // 256 + 1; y and z lie between 0 and 4. `padded_partner_list`: slots in the numbering of the steps; entries past active_partner_number are padding. `active_partner_number`: the first atom of every domain has 64 live slots. `exported_site_indices`: the 128 entries of a domain are distinct local atom numbers; the first 64 go to the domain before, the others to the domain after. `fourier_modes`: distinct triples; the first component is 1 to 48, the others -8 to 7.
All inputs are finite; a program needn't handle non-finite values.
Results may differ from the reference program's by a relative error of at most 0.0034.
Values may be sent and summed in bfloat16 or wider, within the bound.
A program may use at most 64 MiB of HBM per device.

```python
import math
import jax
import jax.numpy as jnp
from jax import lax

A_DEV = 256
NB = 64
C = 128
HID = 128
NRBF = 16
QCH = 16
KVEC = 12288
HALO = 64
ATOMS = 4096
N_DOM = 16


CELL_SIDE = 4.0


def draw_cartesian_places(key, part):
    key = jax.random.fold_in(key, 7)
    slab_index = (jnp.arange(ATOMS, dtype=jnp.int32) // A_DEV).astype(jnp.float32)
    uniform_draw = jax.random.uniform(key, (3, ATOMS), jnp.float32, 0.0, 0.999)
    along_x = slab_index + uniform_draw[0]
    return jnp.stack([along_x, CELL_SIDE * uniform_draw[1], CELL_SIDE * uniform_draw[2]]).astype(jnp.float32)


def draw_node_descriptors(key, part):
    key = jax.random.fold_in(key, 11)
    row_key, mean_key, scale_key = jax.random.split(key, 3)
    ramp = 0.5 + jnp.arange(ATOMS, dtype=jnp.float32)[:, None] / ATOMS
    centre = jnp.clip(jax.random.normal(mean_key, (1, C), jnp.float32), -2.0, 2.0)
    noise = jnp.clip(jax.random.normal(row_key, (ATOMS, C), jnp.float32), -4.0, 4.0)
    values = noise + ramp * centre
    return values.astype(jnp.bfloat16)


def draw_padded_partner_list(key, part):
    key = jax.random.fold_in(key, 13)
    return jax.random.randint(key, (ATOMS, NB), 0, A_DEV + 2 * HALO).astype(jnp.int32)


def draw_active_partner_number(key, part):
    key = jax.random.fold_in(key, 17)
    counts = jax.random.randint(key, (ATOMS,), NB // 2, NB + 1).astype(jnp.int32)
    return counts.at[::A_DEV].set(NB)


def draw_exported_site_indices(key, part):
    key = jax.random.fold_in(key, 19)
    domain_keys = jax.random.split(key, ATOMS // A_DEV)
    shuffled = jax.vmap(lambda one_key: jax.random.permutation(one_key, A_DEV)[:2 * HALO])(domain_keys)
    return shuffled.reshape(-1).astype(jnp.int32)


def draw_fourier_modes(key, part):
    key = jax.random.fold_in(key, 23)
    shuffled = jax.random.permutation(key, 12288)[:KVEC].astype(jnp.int32)
    first_comp = shuffled // 256 + 1
    second_comp = shuffled // 16 % 16 - 8
    third_comp = shuffled % 16 - 8
    return jnp.stack([first_comp, second_comp, third_comp]).astype(jnp.int32)


def centred(stream_key, shape, scale, reach, kind=jnp.bfloat16):
    drawn = jax.random.normal(stream_key, shape, jnp.float32) * scale
    return jnp.minimum(jnp.maximum(drawn, -reach), reach).astype(kind)


def setup_inputs(seed: int = 0, part: int = 0) -> dict:
    arg_keys = jax.random.split(jax.random.key(seed), 12)
    own_keys = jax.random.split(jax.random.fold_in(arg_keys[11], part), 12)
    cartesian_places = draw_cartesian_places(jax.random.fold_in(jax.random.fold_in(arg_keys[11], part), 71), part)
    node_descriptors = draw_node_descriptors(jax.random.fold_in(jax.random.fold_in(arg_keys[11], part), 71), part)
    padded_partner_list = draw_padded_partner_list(jax.random.fold_in(jax.random.fold_in(arg_keys[11], part), 71), part)
    active_partner_number = draw_active_partner_number(jax.random.fold_in(jax.random.fold_in(arg_keys[11], part), 71), part)
    exported_site_indices = draw_exported_site_indices(jax.random.fold_in(jax.random.fold_in(arg_keys[11], part), 71), part)
    fourier_modes = draw_fourier_modes(jax.random.fold_in(arg_keys[11], 71), part)
    hidden_pole_projection = centred(arg_keys[6], (C, QCH), C ** -0.5, 0.5)
    distance_mlp_first_matrix = centred(arg_keys[7], (NRBF, HID), NRBF ** -0.5, 1.5)
    distance_mlp_second_matrix = centred(arg_keys[8], (HID, HID), HID ** -0.5, 0.5)
    distance_mlp_final_matrix = centred(arg_keys[9], (HID, C), HID ** -0.5, 0.5)
    energy_projection = centred(arg_keys[10], (C,), 1.0, 4.0, jnp.float32)
    return dict(cartesian_places=cartesian_places, node_descriptors=node_descriptors, padded_partner_list=padded_partner_list, active_partner_number=active_partner_number, exported_site_indices=exported_site_indices, fourier_modes=fourier_modes, hidden_pole_projection=hidden_pole_projection, distance_mlp_first_matrix=distance_mlp_first_matrix, distance_mlp_second_matrix=distance_mlp_second_matrix, distance_mlp_final_matrix=distance_mlp_final_matrix, energy_projection=energy_projection)


CELL_SIDE = 4.0
PREC_HIGH = lax.Precision.HIGHEST
CONTRACT_FIRST = (((0,), (0,)), ((), ()))
CONTRACT_LAST = (((1,), (1,)), ((), ()))


def decay_table(rate_count):
    return 0.02 * 64.0 ** (jnp.arange(rate_count, dtype=jnp.float32) / (rate_count - 1))


def silu_slope(values):
    logistic = jax.nn.sigmoid(values)
    return logistic * (1.0 + values * (1.0 - logistic))


def mode_lookup_array(fourier_modes, cubic_cell_side):
    lattice_sum_coefficients = jnp.array([2.0 * math.pi / cubic_cell_side, 2.0 * math.pi / CELL_SIDE, 2.0 * math.pi / CELL_SIDE], jnp.float32)
    fourier_space_modes = fourier_modes.astype(jnp.float32) * lattice_sum_coefficients[:, None]
    ksquare = jnp.sum(fourier_space_modes * fourier_space_modes, 0)
    mode_coefficient = 4.0 * jnp.exp(-ksquare / 1024.0) / (ksquare + 0.25)
    return fourier_space_modes, mode_coefficient


def phase_pair(coords, wave_part):
    phase_angle = coords[0][:, None] * wave_part[0][None, :] + coords[1][:, None] * wave_part[1][None, :]
    phase_angle = phase_angle + coords[2][:, None] * wave_part[2][None, :]
    return jnp.cos(phase_angle), jnp.sin(phase_angle)


def edge_terms(separation, edge_mask, partner_feats, decay_rates, distance_mlp_first_matrix, distance_mlp_second_matrix, distance_mlp_final_matrix, energy_projection):
    atom_rows, slot_count = edge_mask.shape
    edge_total = atom_rows * slot_count
    edge_scale = slot_count ** -0.5
    squared = jnp.sum(separation * separation, 0).reshape(edge_total)
    radial_basis = jnp.exp(-decay_rates[:, None] * squared[None, :])
    pre_one = lax.dot_general(radial_basis.astype(jnp.bfloat16), distance_mlp_first_matrix, CONTRACT_FIRST, preferred_element_type=jnp.float32)
    hidden_one = jax.nn.silu(pre_one).astype(jnp.bfloat16)
    pre_two = jnp.dot(hidden_one, distance_mlp_second_matrix, preferred_element_type=jnp.float32)
    hidden_two = jax.nn.silu(pre_two).astype(jnp.bfloat16)
    filters = jnp.dot(hidden_two, distance_mlp_final_matrix, preferred_element_type=jnp.float32)
    live_edges = edge_mask.reshape(edge_total, 1).astype(jnp.float32)
    feats_wide = partner_feats.astype(jnp.float32)
    weighted = live_edges * filters
    message = edge_scale * jnp.sum((weighted * feats_wide).reshape(atom_rows, slot_count, -1), 1)
    out_slope = energy_projection[None, :] * silu_slope(message)
    slope_edges = jnp.repeat(out_slope, slot_count, 0)
    filter_grad = (edge_scale * live_edges * slope_edges * feats_wide).astype(jnp.bfloat16)
    grad_two = lax.dot_general(filter_grad, distance_mlp_final_matrix, CONTRACT_LAST, preferred_element_type=jnp.float32)
    pre_grad_two = (grad_two * silu_slope(pre_two)).astype(jnp.bfloat16)
    grad_one = lax.dot_general(pre_grad_two, distance_mlp_second_matrix, CONTRACT_LAST, preferred_element_type=jnp.float32)
    pre_grad_one = (grad_one * silu_slope(pre_one)).astype(jnp.bfloat16)
    basis_grad = lax.dot_general(distance_mlp_first_matrix, pre_grad_one, CONTRACT_LAST, preferred_element_type=jnp.float32)
    square_grad = -jnp.sum(decay_rates[:, None] * radial_basis * basis_grad, 0)
    pair_grad = 2.0 * square_grad.reshape(atom_rows, slot_count)[None] * separation
    feat_grad = edge_scale * weighted * slope_edges
    return pair_grad, feat_grad


def long_factors(coords, charges, fourier_space_modes, kblock):
    number_of_modes = fourier_space_modes.shape[1]

    def factor_block(carry, block_index):
        first_wave = (block_index * kblock).astype(jnp.int32)
        wave_part = lax.dynamic_slice_in_dim(fourier_space_modes, first_wave, kblock, 1)
        cosines, sines = phase_pair(coords, wave_part)
        real_part = lax.dot_general(charges, cosines, CONTRACT_FIRST, precision=PREC_HIGH, preferred_element_type=jnp.float32)
        imag_part = lax.dot_general(charges, sines, CONTRACT_FIRST, precision=PREC_HIGH, preferred_element_type=jnp.float32)
        return carry, (real_part, imag_part)

    _, stacked = lax.scan(factor_block, None, jnp.arange(number_of_modes // kblock, dtype=jnp.int32))
    real_all = stacked[0].transpose(1, 0, 2).reshape(charges.shape[1], number_of_modes)
    imag_all = stacked[1].transpose(1, 0, 2).reshape(charges.shape[1], number_of_modes)
    return real_all, imag_all


def long_backward(coords, charges, fourier_space_modes, real_grad, imag_grad, kblock):
    atom_count = coords.shape[1]

    def force_block(carry, block_index):
        force_acc, charge_acc = carry
        first_wave = (block_index * kblock).astype(jnp.int32)
        wave_part = lax.dynamic_slice_in_dim(fourier_space_modes, first_wave, kblock, 1)
        cosines, sines = phase_pair(coords, wave_part)
        real_slice = lax.dynamic_slice_in_dim(real_grad, first_wave, kblock, 1)
        imag_slice = lax.dynamic_slice_in_dim(imag_grad, first_wave, kblock, 1)
        along_real = jnp.dot(charges, real_slice, precision=PREC_HIGH, preferred_element_type=jnp.float32)
        along_imag = jnp.dot(charges, imag_slice, precision=PREC_HIGH, preferred_element_type=jnp.float32)
        dphase = cosines * along_imag - sines * along_real
        force_acc = force_acc + lax.dot_general(wave_part, dphase, CONTRACT_LAST, precision=PREC_HIGH, preferred_element_type=jnp.float32)
        charge_acc = charge_acc + lax.dot_general(cosines, real_slice, CONTRACT_LAST, precision=PREC_HIGH, preferred_element_type=jnp.float32)
        charge_acc = charge_acc + lax.dot_general(sines, imag_slice, CONTRACT_LAST, precision=PREC_HIGH, preferred_element_type=jnp.float32)
        return (force_acc, charge_acc), None

    initial = (jnp.zeros((3, atom_count), jnp.float32), jnp.zeros((atom_count, real_grad.shape[0]), jnp.float32))
    (force_acc, charge_acc), _ = lax.scan(force_block, initial, jnp.arange(real_grad.shape[1] // kblock, dtype=jnp.int32))
    return force_acc, charge_acc


def reference(cartesian_places, node_descriptors, padded_partner_list, active_partner_number, exported_site_indices, fourier_modes, hidden_pole_projection, distance_mlp_first_matrix, distance_mlp_second_matrix, distance_mlp_final_matrix, energy_projection):
    cubic_cell_side = float(N_DOM)
    decay_rates = decay_table(NRBF)
    atom_block = math.gcd(ATOMS, max(1, 1024 // NB))
    slot_ids = jnp.arange(NB, dtype=jnp.int32)

    def edge_block(carry, block_index):
        grad_pos, grad_feat = carry
        first_row = (block_index * atom_block).astype(jnp.int32)
        owners = first_row + jnp.arange(atom_block, dtype=jnp.int32)
        nbr_slots = lax.dynamic_slice_in_dim(padded_partner_list, first_row, atom_block, 0)
        counts = lax.dynamic_slice_in_dim(active_partner_number, first_row, atom_block, 0)
        domain = (owners // A_DEV)[:, None]
        left_domain = (domain + N_DOM - 1) % N_DOM
        right_domain = (domain + 1) % N_DOM
        from_left = (nbr_slots >= A_DEV) & (nbr_slots < A_DEV + HALO)
        from_right = nbr_slots >= A_DEV + HALO
        left_pick = jnp.clip(nbr_slots - A_DEV, 0, HALO - 1)
        right_pick = jnp.clip(nbr_slots - A_DEV - HALO, 0, HALO - 1)
        left_atom = left_domain * A_DEV + exported_site_indices[left_domain * (2 * HALO) + HALO + left_pick]
        right_atom = right_domain * A_DEV + exported_site_indices[right_domain * (2 * HALO) + right_pick]
        local_atom = domain * A_DEV + jnp.minimum(nbr_slots, A_DEV - 1)
        partner = jnp.where(from_left, left_atom, jnp.where(from_right, right_atom, local_atom)).astype(jnp.int32)
        image_shift = jnp.where(from_left & (domain == 0), -cubic_cell_side, 0.0) + jnp.where(from_right & (domain == N_DOM - 1), cubic_cell_side, 0.0)
        near = cartesian_places[:, partner]
        near = near.at[0].add(image_shift.astype(jnp.float32))
        own_coords = cartesian_places[:, owners]
        separation = near - own_coords[:, :, None]
        edge_mask = slot_ids[None, :] < counts[:, None]
        partner_flat = partner.reshape(-1)
        pair_grad, feat_grad = edge_terms(separation, edge_mask, node_descriptors[partner_flat], decay_rates, distance_mlp_first_matrix, distance_mlp_second_matrix, distance_mlp_final_matrix, energy_projection)
        grad_pos = grad_pos.at[:, partner_flat].add(pair_grad.reshape(3, -1))
        grad_pos = grad_pos.at[:, owners].add(-jnp.sum(pair_grad, 2))
        grad_feat = grad_feat.at[partner_flat].add(feat_grad)
        return (grad_pos, grad_feat), None

    initial = (jnp.zeros((3, ATOMS), jnp.float32), jnp.zeros((ATOMS, C), jnp.float32))
    (grad_pos, grad_feat), _ = lax.scan(edge_block, initial, jnp.arange(ATOMS // atom_block, dtype=jnp.int32))

    fourier_space_modes, mode_coefficient = mode_lookup_array(fourier_modes, cubic_cell_side)
    charges_raw = jnp.dot(node_descriptors, hidden_pole_projection, preferred_element_type=jnp.float32)
    charges = charges_raw - jnp.mean(charges_raw, 0)
    coupling = float(ATOMS * KVEC) ** -0.5
    kblock = math.gcd(KVEC, 512)
    real_sf, imag_sf = long_factors(cartesian_places, charges, fourier_space_modes, kblock)
    real_grad = (2.0 * coupling) * mode_coefficient[None, :] * real_sf
    imag_grad = (2.0 * coupling) * mode_coefficient[None, :] * imag_sf
    long_grad, charge_grad = long_backward(cartesian_places, charges, fourier_space_modes, real_grad, imag_grad, kblock)
    raw_grad = charge_grad - jnp.mean(charge_grad, 0)
    feat_long = jnp.dot(raw_grad, hidden_pole_projection.astype(jnp.float32).T, precision=PREC_HIGH, preferred_element_type=jnp.float32)
    forces = -(grad_pos + long_grad)
    feature_grad = (grad_feat + feat_long).astype(jnp.bfloat16)
    return (forces, feature_grad)
```

```python
import functools
import math

import jax
import jax.numpy as jnp
from jax import lax
from jax.experimental import pallas as pl
from jax.experimental.pallas import tpu as pltpu
from jax.sharding import PartitionSpec as P

CELL_SIDE = 4.0
PREC_HIGH = lax.Precision.HIGHEST
F32 = jnp.float32
BF16 = jnp.bfloat16
NT = (((1,), (1,)), ((), ()))
NN = (((1,), (0,)), ((), ()))
TN = (((0,), (0,)), ((), ()))
MODES_X = 48
MODES_Y = 16
MODES_Z = 16


def dotf(a, b, dims=NN):
    return lax.dot_general(a, b, dims, preferred_element_type=F32)


def split2(a):
    hi = a.astype(BF16)
    return hi, (a - hi.astype(F32)).astype(BF16)


def split3(a):
    hi = lax.reduce_precision(a, 8, 7)
    mid = lax.reduce_precision(a - hi, 8, 7)
    return hi.astype(BF16), mid.astype(BF16), (a - hi - mid).astype(BF16)


def dot3(a, b, dims):
    ah, al = a
    bh, bl = b
    return dotf(ah, bh, dims) + (dotf(al, bh, dims) + dotf(ah, bl, dims))


def sincos_turns(turns):
    x = (turns - jnp.round(turns)) * (2.0 * math.pi)
    x2 = x * x
    c = jnp.full_like(x, 1.0 / math.factorial(16))
    for n in range(14, -1, -2):
        c = c * x2 + (-1.0) ** (n // 2) / math.factorial(n)
    s = jnp.full_like(x, 1.0 / math.factorial(17))
    for n in range(15, 0, -2):
        s = s * x2 + (-1.0) ** (n // 2) / math.factorial(n)
    return c, s * x


def edge_kernel(slots, idx_ref, table_ref, own_ref, w1t_ref, w1_ref, w2t_ref, w2_ref, w3t_ref, w3_ref, eproj_ref, decay_ref, acc_ref, own_out_ref):
    edges = idx_ref.shape[2]
    atoms = own_ref.shape[2]
    rows = table_ref.shape[1]
    scale = slots ** (-0.5)
    chan = w3t_ref.shape[0]

    @pl.when(pl.program_id(0) == 0)
    def _():
        acc_ref[...] = jnp.zeros_like(acc_ref)

    idx = idx_ref[0]
    one = jnp.where(lax.broadcasted_iota(jnp.int32, (rows, edges), 0) == idx, 1.0, 0.0).astype(BF16)
    first = lax.broadcasted_iota(jnp.int32, (atoms, edges), 0) * slots
    edge_id = lax.broadcasted_iota(jnp.int32, (atoms, edges), 1)
    owner = jnp.where((edge_id >= first) & (edge_id < first + slots), 1.0, 0.0).astype(BF16)
    got = dotf(table_ref[...], one)
    feats = got[:chan]
    own = dotf(own_ref[0], owner)
    sep = got[chan : chan + 8]
    sep = sep - own[0:8]
    for n in (8, 16):
        sep = sep + (got[chan + n : chan + n + 8] - own[n : n + 8])
    sep = sep + got[chan + 24 : chan + 32]
    sq = jnp.sum(sep * sep, 0, keepdims=True)
    decay = decay_ref[...]
    basis = jnp.exp(-decay * sq)
    pre1 = dotf(w1t_ref[...], basis.astype(BF16))
    sig1 = 0.5 * jnp.tanh(0.5 * pre1) + 0.5
    h1 = pre1 * sig1
    slope1 = sig1 + h1 * (1.0 - sig1)
    pre2 = dotf(w2t_ref[...], h1.astype(BF16))
    sig2 = 0.5 * jnp.tanh(0.5 * pre2) + 0.5
    h2 = pre2 * sig2
    slope2 = sig2 + h2 * (1.0 - sig2)
    filters = dotf(w3t_ref[...], h2.astype(BF16))
    prod_hi, prod_lo = split2(filters * feats)
    message = scale * (dotf(prod_hi, owner, NT) + dotf(prod_lo, owner, NT))
    sigm = 1.0 / (1.0 + jnp.exp(-message))
    out_slope = scale * eproj_ref[...] * (sigm * (1.0 + message * (1.0 - sigm)))
    os_hi, os_lo = split2(out_slope)
    slope_e = dotf(os_hi, owner) + dotf(os_lo, owner)
    fgrad = (slope_e * feats).astype(BF16)
    g2 = (dotf(w3_ref[...], fgrad) * slope2).astype(BF16)
    g1 = (dotf(w2_ref[...], g2) * slope1).astype(BF16)
    bg = dotf(w1_ref[...], g1)
    sgrad = -2.0 * jnp.sum(decay * basis * bg, 0, keepdims=True)
    pair = sgrad * sep
    pair_hi, pair_lo = split2(pair)
    pairs = jnp.concatenate([pair_hi, pair_lo], 0)
    acc_ref[0:chan, :] += dotf((filters * slope_e).astype(BF16), one, NT)
    acc_ref[chan:, :] += dotf(pairs, one, NT)
    own_out_ref[0] = dotf(pairs, owner, NT)


def long_kernel(nk, inv_side, data_ref, mean_ref, kp_ref, wave_ref, wt_ref, out_ref, sf_ref, mh_ref, ml_ref):
    phase = pl.program_id(0)
    block = pl.program_id(1)
    mp = kp_ref.shape[1]
    chan = mean_ref.shape[0]
    nb = data_ref.shape[1]
    q = data_ref[0:chan, :] - mean_ref[...]
    x = data_ref[chan : chan + 1, :] * inv_side
    y = data_ref[chan + 1 : chan + 2, :] * (1.0 / CELL_SIDE)
    z = data_ref[chan + 2 : chan + 3, :] * (1.0 / CELL_SIDE)
    ec, es = sincos_turns(kp_ref[0] * x + kp_ref[1] * y)
    k2 = lax.broadcasted_iota(jnp.int32, (MODES_Z, 1), 0).astype(F32) - float(MODES_Z // 2)
    zc, zs = sincos_turns(k2 * z)
    half = chan * MODES_Z
    a_re = (q[:, None, :] * zc[None, :, :]).reshape(half, nb)
    a_im = (q[:, None, :] * zs[None, :, :]).reshape(half, nb)
    acat = split2(jnp.concatenate([a_re, a_im], 0))
    ecat = split2(jnp.concatenate([ec, es], 0))

    @pl.when((phase == 0) & (block == 0))
    def _():
        sf_ref[...] = jnp.zeros_like(sf_ref)

    @pl.when(phase == 0)
    def _():
        sf_ref[...] += dot3(acat, ecat, NT)

    @pl.when((phase == 0) & (block == nk - 1))
    def _():
        s = sf_ref[...]
        wt = wt_ref[...]
        re = wt * (s[:half, :mp] - s[half:, mp:])
        im = wt * (s[:half, mp:] + s[half:, :mp])
        m = jnp.concatenate(
            [jnp.concatenate([re, im], 1), jnp.concatenate([im, -re], 1)], 0
        )
        hi, lo = split2(m)
        mh_ref[...] = hi
        ml_ref[...] = lo

    @pl.when(phase == 1)
    def _():
        m = (mh_ref[...], ml_ref[...])
        u = dot3(m, ecat, NN)
        ur = u[:half].reshape(chan, MODES_Z, nb)
        ui = u[half:].reshape(chan, MODES_Z, nb)
        cg = jnp.sum(zc[None] * ur + zs[None] * ui, 1)
        kz = k2 * (2.0 * math.pi / CELL_SIDE)
        lz = jnp.sum((kz * zc)[None] * ui - (kz * zs)[None] * ur, 1)
        lz = jnp.sum(q * lz, 0, keepdims=True)
        p = dot3(m, acat, TN)
        dp = ec * p[mp:] - es * p[:mp]
        lx = jnp.sum(wave_ref[0] * dp, 0, keepdims=True)
        ly = jnp.sum(wave_ref[1] * dp, 0, keepdims=True)
        out_ref[0:chan, :] = cg
        out_ref[chan:, :] = jnp.concatenate([lx, ly, lz, jnp.zeros((5, nb), F32)], 0)


def long_range(places, nodes_t, proj, side, modes):
    n = lax.axis_size("dom")
    here = places.shape[1]
    chan = proj.shape[1]
    total = n * here
    raw = dotf(proj.T, nodes_t)
    mine = jnp.concatenate([raw, places, jnp.zeros((5, here), F32)], 0)
    data = lax.all_gather(mine, "dom", axis=1, tiled=True)
    mean = jnp.sum(data[:chan], 1, keepdims=True) / total
    pairs = MODES_X * MODES_Y
    m = -(-pairs // n)
    mp = -(-m // 8) * 8
    local_p = jnp.arange(mp, dtype=jnp.int32)
    flat = lax.axis_index("dom") * m + local_p
    real = (local_p < m) & (flat < pairs)
    k0 = (flat // MODES_Y + 1).astype(F32)
    k1 = (flat % MODES_Y - MODES_Y // 2).astype(F32)
    kx, ky = k0 * (2.0 * math.pi / side), k1 * (2.0 * math.pi / CELL_SIDE)
    kz = (jnp.arange(MODES_Z) - MODES_Z // 2).astype(F32) * (2.0 * math.pi / CELL_SIDE)
    ksq = (kx * kx + ky * ky)[None, :] + (kz * kz)[:, None]
    coupling = float(total * modes) ** (-0.5)
    wt = 2.0 * coupling * 4.0 * jnp.exp(-ksq / 1024.0) / (ksq + 0.25)
    wt = jnp.where(real[None, :], wt, 0.0)
    wt = jnp.tile(wt, (chan, 1))
    kp = jnp.stack([k0, k1])[:, :, None]
    wave = jnp.stack([kx, ky])[:, :, None]
    nb = math.gcd(total, 512)
    nk = total // nb
    half = chan * MODES_Z
    whole = lambda shape: pl.BlockSpec(shape, lambda a, b: (0,) * len(shape))
    rows = data.shape[0]
    out = pl.pallas_call(
        functools.partial(long_kernel, nk, 1.0 / side),
        out_shape=jax.ShapeDtypeStruct((rows, total), F32),
        grid=(2, nk),
        in_specs=[
            pl.BlockSpec((rows, nb), lambda a, b: (0, b)),
            whole((chan, 1)),
            whole((2, mp, 1)),
            whole((2, mp, 1)),
            whole((half, mp)),
        ],
        out_specs=pl.BlockSpec((rows, nb), lambda a, b: (0, a * b)),
        scratch_shapes=[
            pltpu.VMEM((2 * half, 2 * mp), F32),
            pltpu.VMEM((2 * half, 2 * mp), BF16),
            pltpu.VMEM((2 * half, 2 * mp), BF16),
        ],
        compiler_params=pltpu.CompilerParams(vmem_limit_bytes=40 * 2**20),
        cost_estimate=pl.CostEstimate(flops=4 * 10**9, bytes_accessed=2 * 10**6, transcendentals=0),
        name="long_range",
    )(data, mean, kp, wave, wt)
    sums = jnp.sum(out[:chan], 1)
    line = jnp.tile(jnp.pad(sums, (0, here - chan)), n)[None]
    out = jnp.concatenate([out[: chan + 3], line, out[chan + 4 :]], 0)
    mine = lax.psum_scatter(out, "dom", scatter_dimension=1, tiled=True)
    charge_grad = mine[:chan]
    raw_grad = charge_grad - mine[chan + 3, :chan][:, None] / total
    return mine[chan : chan + 3], raw_grad


def shift_pair(to_prev, to_next):
    n = lax.axis_size("dom")
    forward = [(i, (i + 1) % n) for i in range(n)]
    backward = [(t, s) for s, t in forward]
    from_prev = lax.ppermute(to_next, "dom", forward)
    from_next = lax.ppermute(to_prev, "dom", backward)
    return from_prev, from_next


def local(places, nodes, partners, counts, exported, modes, proj, w1, w2, w3, eproj):
    n = lax.axis_size("dom")
    me = lax.axis_index("dom")
    here, chan = nodes.shape
    halo = exported.shape[0] // 2
    slots = partners.shape[1]
    side = float(n)
    nrbf = w1.shape[0]
    nodes_t = nodes.T

    pad8 = lambda a: jnp.pad(a, ((0, 5), (0, 0)))
    parts = jnp.concatenate([pad8(a) for a in split3(places)], 0)
    mine = jnp.concatenate([nodes_t, parts], 0)
    pick = (jnp.arange(here, dtype=jnp.int32)[:, None] == exported[None, :]).astype(BF16)
    sent = dotf(mine, pick).astype(BF16)
    left, right = shift_pair(sent[:, :halo], sent[:, halo:])
    table = jnp.concatenate([mine, left, right], 1)
    col = jnp.arange(here + 2 * halo)
    shift = jnp.where((col >= here) & (col < here + halo) & (me == 0), -side, 0.0)
    shift = shift + jnp.where((col >= here + halo) & (me == n - 1), side, 0.0)
    table = jnp.concatenate([table, jnp.pad(shift[None].astype(BF16), ((0, 7), (0, 0)))], 0)

    long_grad, raw_grad = long_range(places, nodes_t, proj, side, modes.shape[1])

    blk = math.gcd(here, 32)
    nblk = here // blk
    edges = blk * slots
    live = jnp.arange(slots, dtype=jnp.int32)[None, :] < counts[:, None]
    idx = jnp.where(live, partners, -1).reshape(nblk, 1, edges)
    own = parts.reshape(24, nblk, blk).transpose(1, 0, 2)
    decay = (0.02 * 64.0 ** (jnp.arange(nrbf, dtype=F32) / (nrbf - 1)))[:, None]
    rows = table.shape[1]
    whole = lambda a: pl.BlockSpec(a.shape, lambda i: (0,) * a.ndim)
    fixed = [w1.T, w1, w2.T, w2, w3.T, w3, eproj[:, None], decay]
    acc, own_out = pl.pallas_call(
        functools.partial(edge_kernel, slots),
        out_shape=(
            jax.ShapeDtypeStruct((chan + 16, rows), F32),
            jax.ShapeDtypeStruct((nblk, 16, blk), F32),
        ),
        grid=(nblk,),
        in_specs=[
            pl.BlockSpec((1, 1, edges), lambda i: (i, 0, 0)),
            whole(table),
            pl.BlockSpec((1, 24, blk), lambda i: (i, 0, 0)),
        ]
        + [whole(a) for a in fixed],
        out_specs=(
            pl.BlockSpec((chan + 16, rows), lambda i: (0, 0)),
            pl.BlockSpec((1, 16, blk), lambda i: (i, 0, 0)),
        ),
        compiler_params=pltpu.CompilerParams(vmem_limit_bytes=48 * 2**20),
        cost_estimate=pl.CostEstimate(flops=8 * 10**9, bytes_accessed=2 * 10**6, transcendentals=0),
        name="edges",
    )(idx, table, own, *fixed)
    own_sum = own_out.transpose(1, 0, 2).reshape(16, here)
    grads = jnp.concatenate([acc[:chan], acc[chan : chan + 8] + acc[chan + 8 :]], 0)
    back_left, back_right = shift_pair(grads[:, here : here + halo], grads[:, here + halo :])
    returned = jnp.concatenate([back_left, back_right], 1)
    return finish(grads, returned, own_sum, pick, long_grad, raw_grad, proj, here, chan)


def finish(grads, returned, own_sum, pick, long_grad, raw_grad, proj, here, chan):
    back = lax.dot_general(returned, pick.astype(F32), NT, precision=PREC_HIGH, preferred_element_type=F32)
    grads = grads[:, :here] + back
    short_grad = grads[chan : chan + 3] - own_sum[0:3] - own_sum[8:11]
    forces = -(short_grad + long_grad)
    feat_long = lax.dot_general(proj.astype(F32), raw_grad, NN, precision=PREC_HIGH, preferred_element_type=F32)
    feature_grad = (grads[:chan] + feat_long).T.astype(BF16)
    return (forces, feature_grad)


def solution(mesh):
    both = ("groups", "dom")
    in_specs = (P(None, both), P(both, None), P(both, None), P(both), P(both)) + (P(),) * 6
    out_specs = (P(None, both), P(both, None))
    return jax.shard_map(local, mesh=mesh, in_specs=in_specs, out_specs=out_specs, check_vma=False)
```

```python
import functools
import math

import jax
import jax.numpy as jnp
from jax import lax
from jax.experimental import pallas as pl
from jax.experimental.pallas import tpu as pltpu
from jax.sharding import PartitionSpec as P

CELL_SIDE = 4.0
PREC_HIGH = lax.Precision.HIGHEST
F32 = jnp.float32
BF16 = jnp.bfloat16
NT = (((1,), (1,)), ((), ()))
NN = (((1,), (0,)), ((), ()))
TN = (((0,), (0,)), ((), ()))
MODES_X = 48
MODES_Y = 16
MODES_Z = 16


def dotf(a, b, dims=NN):
    return lax.dot_general(a, b, dims, preferred_element_type=F32)


def split2(a):
    hi = a.astype(BF16)
    return hi, (a - hi.astype(F32)).astype(BF16)


def split3(a):
    hi = lax.reduce_precision(a, 8, 7)
    mid = lax.reduce_precision(a - hi, 8, 7)
    return hi.astype(BF16), mid.astype(BF16), (a - hi - mid).astype(BF16)


def dot3(a, b, dims):
    ah, al = a
    bh, bl = b
    return dotf(ah, bh, dims) + (dotf(al, bh, dims) + dotf(ah, bl, dims))


def sincos_turns(turns):
    x = (turns - jnp.round(turns)) * (2.0 * math.pi)
    x2 = x * x
    c = jnp.full_like(x, 1.0 / math.factorial(16))
    for n in range(14, -1, -2):
        c = c * x2 + (-1.0) ** (n // 2) / math.factorial(n)
    s = jnp.full_like(x, 1.0 / math.factorial(17))
    for n in range(15, 0, -2):
        s = s * x2 + (-1.0) ** (n // 2) / math.factorial(n)
    return c, s * x


def edge_block(slots, idx, own_parts, table, weights, one, owner):
    w1t_ref, w1_ref, w2t_ref, w2_ref, w3t_ref, w3_ref, eproj_ref, decay_ref = weights
    scale = slots ** (-0.5)
    chan = w3t_ref.shape[0]
    got = dotf(table, one)
    feats = got[:chan]
    own = dotf(own_parts, owner)
    sep = got[chan : chan + 8] - own[0:8]
    for n in (8, 16):
        sep = sep + (got[chan + n : chan + n + 8] - own[n : n + 8])
    sep = sep + got[chan + 24 : chan + 32]
    sq = jnp.sum(sep * sep, 0, keepdims=True)
    decay = decay_ref[...]
    basis = jnp.exp(-decay * sq)
    pre1 = dotf(w1t_ref[...], basis.astype(BF16))
    sig1 = 0.5 * jnp.tanh(0.5 * pre1) + 0.5
    h1 = pre1 * sig1
    slope1 = sig1 + h1 * (1.0 - sig1)
    pre2 = dotf(w2t_ref[...], h1.astype(BF16))
    sig2 = 0.5 * jnp.tanh(0.5 * pre2) + 0.5
    h2 = pre2 * sig2
    slope2 = sig2 + h2 * (1.0 - sig2)
    filters = dotf(w3t_ref[...], h2.astype(BF16))
    prod_hi, prod_lo = split2(filters * feats)
    message = scale * (dotf(prod_hi, owner, NT) + dotf(prod_lo, owner, NT))
    sigm = 1.0 / (1.0 + jnp.exp(-message))
    out_slope = scale * eproj_ref[...] * (sigm * (1.0 + message * (1.0 - sigm)))
    os_hi, os_lo = split2(out_slope)
    slope_e = dotf(os_hi, owner) + dotf(os_lo, owner)
    fgrad = (slope_e * feats).astype(BF16)
    g2 = (dotf(w3_ref[...], fgrad) * slope2).astype(BF16)
    g1 = (dotf(w2_ref[...], g2) * slope1).astype(BF16)
    bg = dotf(w1_ref[...], g1)
    sgrad = -2.0 * jnp.sum(decay * basis * bg, 0, keepdims=True)
    pair_hi, pair_lo = split2(sgrad * sep)
    pairs = jnp.concatenate([pair_hi, pair_lo], 0)
    feat_part = dotf((filters * slope_e).astype(BF16), one, NT)
    pos_part = dotf(pairs, one, NT)
    own_part = dotf(pairs, owner, NT)
    return feat_part, pos_part[:8] + pos_part[8:], own_part[:8] + own_part[8:]


def layer_kernel(n, slots, inv_side, inv_total, sent_ref, mine_ref, data_ref, idx_ref, own_ref, pick_ref, proj_ref, kp_ref, wave_ref, wt_ref, w1t_ref, w1_ref, w2t_ref, w2_ref, w3t_ref, w3_ref, eproj_ref, decay_ref, feat_ref, pos_ref, own_out_ref, halo, table, gath, acc, ret_send, ret, sf, mh, ml, res_send, res, halo_ss, halo_rs, gath_ss, gath_rs, ret_ss, ret_rs, res_ss, res_rs):
    me = lax.axis_index("dom")
    after, before = lax.rem(me + 1, n), lax.rem(me + n - 1, n)
    mesh_id = pl.DeviceIdType.MESH

    def loop(first, last, body):
        def step(t, carry):
            body(t)
            return carry

        lax.fori_loop(first, last, step, 0)

    def remote(src, dst, ss, rs, target):
        return pltpu.make_async_remote_copy(
            src_ref=src, dst_ref=dst, send_sem=ss, recv_sem=rs, device_id={"dom": target}, device_id_type=mesh_id
        )

    barrier = pltpu.get_barrier_semaphore()
    loop(1, n, lambda t: pl.semaphore_signal(barrier, inc=1, device_id={"dom": lax.rem(me + t, n)}, device_id_type=mesh_id))
    pl.semaphore_wait(barrier, n - 1)

    def halo_copy(k):
        return remote(sent_ref.at[k], halo.at[k], halo_ss.at[k], halo_rs.at[k], (after, before)[k])

    def ret_copy(k):
        return remote(ret_send, ret.at[k], ret_ss.at[k], ret_rs.at[k], (before, after)[k])

    def gath_copy(t):
        return remote(data_ref, gath.at[t], gath_ss.at[t], gath_rs.at[t], lax.rem(me + t, n))

    def res_copy(t):
        return remote(res_send.at[t], res.at[t], res_ss.at[t], res_rs.at[t], lax.rem(me + n - t, n))

    halo_copy(0).start()
    halo_copy(1).start()
    loop(1, n, lambda t: gath_copy(t).start())
    gath[0] = data_ref[...]

    here = mine_ref.shape[1]
    edges = idx_ref.shape[2]
    atoms = own_ref.shape[2]
    rows = table.shape[1]
    wide = w3t_ref.shape[0]
    chan = proj_ref.shape[1]
    weights = (w1t_ref, w1_ref, w2t_ref, w2_ref, w3t_ref, w3_ref, eproj_ref, decay_ref)
    first = lax.broadcasted_iota(jnp.int32, (atoms, edges), 0) * slots
    edge_id = lax.broadcasted_iota(jnp.int32, (atoms, edges), 1)
    owner = jnp.where((edge_id >= first) & (edge_id < first + slots), 1.0, 0.0).astype(BF16)
    table[:, :here] = mine_ref[...]
    acc[...] = jnp.zeros_like(acc)
    halo_copy(0).wait()
    halo_copy(1).wait()
    table[:, here:] = halo[0] + halo[1]

    def edge_step(i):
        one = jnp.where(lax.broadcasted_iota(jnp.int32, (rows, edges), 0) == idx_ref[i], 1.0, 0.0).astype(BF16)
        feat_part, pos_part, own_part = edge_block(slots, idx_ref[i], own_ref[i], table[...], weights, one, owner)
        acc[0:wide, :] += feat_part
        acc[wide:, :] += pos_part
        own_out_ref[i] = own_part

    loop(0, idx_ref.shape[0], edge_step)
    ret_send[...] = acc[:, here:]
    ret_copy(0).start()
    ret_copy(1).start()

    loop(1, n, lambda t: gath_copy(t).wait())
    raw_sum = lax.fori_loop(0, n, lambda t, c: c + gath[t, 0:chan, :], jnp.zeros((chan, here), F32))
    mean = jnp.sum(raw_sum, 1, keepdims=True) * inv_total

    mp = kp_ref.shape[1]
    half = chan * MODES_Z
    k2 = lax.broadcasted_iota(jnp.int32, (MODES_Z, 1), 0).astype(F32) - float(MODES_Z // 2)

    def factors(t):
        q = gath[t, 0:chan, :] - mean
        xyz = gath[t, chan : chan + 8, :]
        x = xyz[0:1] * inv_side
        y = xyz[1:2] * (1.0 / CELL_SIDE)
        z = xyz[2:3] * (1.0 / CELL_SIDE)
        ec, es = sincos_turns(kp_ref[0] * x + kp_ref[1] * y)
        zc, zs = sincos_turns(k2 * z)
        a_re = (q[:, None, :] * zc[None, :, :]).reshape(half, here)
        a_im = (q[:, None, :] * zs[None, :, :]).reshape(half, here)
        return q, ec, es, zc, zs, [a_re, a_im]

    sf[...] = jnp.zeros_like(sf)

    def forward(t):
        q, ec, es, zc, zs, a = factors(t)
        sf[...] += dot3(split2(jnp.concatenate(a + [zc, zs], 0)), split2(jnp.concatenate([ec, es], 0)), NT)

    loop(0, n, forward)
    wt = wt_ref[...]
    re = wt * (sf[:half, :mp] - sf[half : 2 * half, mp:])
    im = wt * (sf[:half, mp:] + sf[half : 2 * half, :mp])
    m1 = 2 * half + MODES_Z
    one_re = sf[2 * half : m1, :mp] - sf[m1:, mp:]
    one_im = sf[2 * half : m1, mp:] + sf[m1:, :mp]
    both = re.reshape(chan, MODES_Z, mp) * one_re[None] + im.reshape(chan, MODES_Z, mp) * one_im[None]
    grad_mean = jnp.sum(jnp.sum(both, 1), 1, keepdims=True) * inv_total
    m = jnp.concatenate([jnp.concatenate([re, im], 1), jnp.concatenate([im, -re], 1)], 0)
    hi, lo = split2(m)
    mh[...] = hi
    ml[...] = lo

    def backward(t):
        q, ec, es, zc, zs, a = factors(t)
        mm = (mh[...], ml[...])
        u = dot3(mm, split2(jnp.concatenate([ec, es], 0)), NN)
        ur = u[:half].reshape(chan, MODES_Z, here)
        ui = u[half:].reshape(chan, MODES_Z, here)
        cg = jnp.sum(zc[None] * ur + zs[None] * ui, 1) - grad_mean
        kz = k2 * (2.0 * math.pi / CELL_SIDE)
        lz = jnp.sum((kz * zc)[None] * ui - (kz * zs)[None] * ur, 1)
        lz = jnp.sum(q * lz, 0, keepdims=True)
        p = dot3(mm, split2(jnp.concatenate(a, 0)), TN)
        dp = ec * p[mp:] - es * p[:mp]
        lx = jnp.sum(wave_ref[0] * dp, 0, keepdims=True)
        ly = jnp.sum(wave_ref[1] * dp, 0, keepdims=True)
        return jnp.concatenate([cg, lx, ly, lz, jnp.zeros((5, here), F32)], 0)

    def send_back(t):
        res_send[t] = backward(t)
        res_copy(t).start()

    loop(1, n, send_back)
    res[0] = backward(0)
    ret_copy(0).wait()
    ret_copy(1).wait()
    back_hi, back_lo = split2(jnp.concatenate([ret[0], ret[1]], 1))
    back = dotf(back_hi, pick_ref[...], NT) + dotf(back_lo, pick_ref[...], NT)
    grads = acc[:, :here] + back
    loop(1, n, lambda t: res_copy(t).wait())
    total = lax.fori_loop(0, n, lambda t, c: c + res[t], jnp.zeros(res.shape[1:], F32))
    raw_hi, raw_lo = split2(total[:chan])
    feat_ref[...] = grads[:wide] + (dotf(proj_ref[...], raw_hi) + dotf(proj_ref[...], raw_lo))
    pos_ref[...] = grads[wide:] + total[chan:]


def local(places, nodes, partners, counts, exported, modes, proj, w1, w2, w3, eproj):
    n = lax.axis_size("dom")
    me = lax.axis_index("dom")
    here, wide = nodes.shape
    halo = exported.shape[0] // 2
    slots = partners.shape[1]
    side = float(n)
    total = n * here
    nrbf = w1.shape[0]
    chan = proj.shape[1]
    nodes_t = nodes.T

    pad8 = lambda a: jnp.pad(a, ((0, 5), (0, 0)))
    parts = jnp.concatenate([pad8(a) for a in split3(places)], 0)
    mine = jnp.concatenate([nodes_t, parts, jnp.zeros((8, here), BF16)], 0)
    order = jnp.concatenate([exported[halo:], exported[:halo]])
    lane = jnp.arange(4 * halo, dtype=jnp.int32)
    keep = (lane < halo) | (lane >= 3 * halo)
    target = jnp.where(keep, jnp.concatenate([order, order]), -1)
    pick = (jnp.arange(here, dtype=jnp.int32)[:, None] == target[None, :]).astype(BF16)
    step = jnp.where((lane < halo) & (me == n - 1), -side, 0.0) + jnp.where((lane >= 3 * halo) & (me == 0), side, 0.0)
    row = jnp.arange(wide + 32, dtype=jnp.int32)[:, None]
    sent = (dotf(mine, pick) + jnp.where(row == wide + 24, step[None, :], 0.0)).astype(BF16)
    sent = jnp.stack([sent[:, : 2 * halo], sent[:, 2 * halo :]])

    data = jnp.concatenate([dotf(proj.T, nodes_t), places, jnp.zeros((5, here), F32)], 0)
    pairs = MODES_X * MODES_Y
    m = -(-pairs // n)
    mp = -(-m // 8) * 8
    local_p = jnp.arange(mp, dtype=jnp.int32)
    flat = me * m + local_p
    real = (local_p < m) & (flat < pairs)
    k0 = (flat // MODES_Y + 1).astype(F32)
    k1 = (flat % MODES_Y - MODES_Y // 2).astype(F32)
    kx, ky = k0 * (2.0 * math.pi / side), k1 * (2.0 * math.pi / CELL_SIDE)
    kz = (jnp.arange(MODES_Z) - MODES_Z // 2).astype(F32) * (2.0 * math.pi / CELL_SIDE)
    ksq = (kx * kx + ky * ky)[None, :] + (kz * kz)[:, None]
    coupling = float(total * modes.shape[1]) ** (-0.5)
    wt = 2.0 * coupling * 4.0 * jnp.exp(-ksq / 1024.0) / (ksq + 0.25)
    wt = jnp.tile(jnp.where(real[None, :], wt, 0.0), (chan, 1))
    kp = jnp.stack([k0, k1])[:, :, None]
    wave = jnp.stack([kx, ky])[:, :, None]
    half = chan * MODES_Z

    blk = math.gcd(here, 32)
    nblk = here // blk
    edges = blk * slots
    live = jnp.arange(slots, dtype=jnp.int32)[None, :] < counts[:, None]
    idx = jnp.where(live, partners, -1).reshape(nblk, 1, edges)
    own = parts.reshape(24, nblk, blk).transpose(1, 0, 2)
    decay = (0.02 * 64.0 ** (jnp.arange(nrbf, dtype=F32) / (nrbf - 1)))[:, None]
    args = [sent, mine, data, idx, own, pick, proj, kp, wave, wt]
    args += [w1.T, w1, w2.T, w2, w3.T, w3, eproj[:, None], decay]
    vmem = pl.BlockSpec(memory_space=pltpu.VMEM)
    dma = pltpu.SemaphoreType.DMA
    borrowed = 2 * halo
    feat, pos, own_out = pl.pallas_call(
        functools.partial(layer_kernel, n, slots, 1.0 / side, 1.0 / total),
        out_shape=(
            jax.ShapeDtypeStruct((wide, here), F32),
            jax.ShapeDtypeStruct((8, here), F32),
            jax.ShapeDtypeStruct((nblk, 8, blk), F32),
        ),
        in_specs=[vmem] * len(args),
        out_specs=(vmem,) * 3,
        scratch_shapes=[
            pltpu.VMEM((2, wide + 32, borrowed), BF16),
            pltpu.VMEM((wide + 32, here + borrowed), BF16),
            pltpu.VMEM((n, chan + 8, here), F32),
            pltpu.VMEM((wide + 8, here + borrowed), F32),
            pltpu.VMEM((wide + 8, borrowed), F32),
            pltpu.VMEM((2, wide + 8, borrowed), F32),
            pltpu.VMEM((2 * half + 2 * MODES_Z, 2 * mp), F32),
            pltpu.VMEM((2 * half, 2 * mp), BF16),
            pltpu.VMEM((2 * half, 2 * mp), BF16),
            pltpu.VMEM((n, chan + 8, here), F32),
            pltpu.VMEM((n, chan + 8, here), F32),
            dma((2,)), dma((2,)), dma((n,)), dma((n,)), dma((2,)), dma((2,)), dma((n,)), dma((n,)),
        ],
        compiler_params=pltpu.CompilerParams(collective_id=0, has_side_effects=True, vmem_limit_bytes=56 * 2**20),
        name="layer",
    )(*args)
    own_sum = own_out.transpose(1, 0, 2).reshape(8, here)
    forces = own_sum[:3] - pos[:3]
    return (forces, feat.T.astype(BF16))


def solution(mesh):
    both = ("groups", "dom")
    in_specs = (P(None, both), P(both, None), P(both, None), P(both), P(both)) + (P(),) * 6
    out_specs = (P(None, both), P(both, None))
    return jax.shard_map(local, mesh=mesh, in_specs=in_specs, out_specs=out_specs, check_vma=False)
```

```python
import functools
import math

import jax
import jax.numpy as jnp
from jax import lax
from jax.experimental import pallas as pl
from jax.experimental.pallas import tpu as pltpu
from jax.sharding import PartitionSpec as P

CELL_SIDE = 4.0
PREC_HIGH = lax.Precision.HIGHEST
F32 = jnp.float32
BF16 = jnp.bfloat16
NT = (((1,), (1,)), ((), ()))
NN = (((1,), (0,)), ((), ()))
TN = (((0,), (0,)), ((), ()))
MODES_X = 48
MODES_Y = 16
MODES_Z = 16


def dotf(a, b, dims=NN):
    return lax.dot_general(a, b, dims, preferred_element_type=F32)


def split2(a):
    hi = a.astype(BF16)
    return hi, (a - hi.astype(F32)).astype(BF16)


def split3(a):
    hi = lax.reduce_precision(a, 8, 7)
    mid = lax.reduce_precision(a - hi, 8, 7)
    return hi.astype(BF16), mid.astype(BF16), (a - hi - mid).astype(BF16)


def dotb(a, b, dims):
    return dotf(a.astype(BF16), b.astype(BF16), dims)


def sincos_turns(turns):
    x = (turns - jnp.round(turns)) * (2.0 * math.pi)
    x2 = x * x
    c = jnp.full_like(x, 1.0 / math.factorial(16))
    for n in range(14, -1, -2):
        c = c * x2 + (-1.0) ** (n // 2) / math.factorial(n)
    s = jnp.full_like(x, 1.0 / math.factorial(17))
    for n in range(15, 0, -2):
        s = s * x2 + (-1.0) ** (n // 2) / math.factorial(n)
    return c, s * x


def edge_block(slots, idx, own_parts, table, weights, one, owner):
    w1t_ref, w1_ref, w2t_ref, w2_ref, w3t_ref, w3_ref, eproj_ref, decay_ref = weights
    scale = slots ** (-0.5)
    chan = w3t_ref.shape[0]
    got = dotf(table, one)
    feats = got[:chan]
    own = dotf(own_parts, owner)
    sep = got[chan : chan + 8] - own[0:8]
    for n in (8, 16):
        sep = sep + (got[chan + n : chan + n + 8] - own[n : n + 8])
    sep = sep + got[chan + 24 : chan + 32]
    sq = jnp.sum(sep * sep, 0, keepdims=True)
    decay = decay_ref[...]
    basis = jnp.exp(-decay * sq)
    pre1 = dotf(w1t_ref[...], basis.astype(BF16))
    sig1 = 0.5 * jnp.tanh(0.5 * pre1) + 0.5
    h1 = pre1 * sig1
    slope1 = sig1 + h1 * (1.0 - sig1)
    pre2 = dotf(w2t_ref[...], h1.astype(BF16))
    sig2 = 0.5 * jnp.tanh(0.5 * pre2) + 0.5
    h2 = pre2 * sig2
    slope2 = sig2 + h2 * (1.0 - sig2)
    filters = dotf(w3t_ref[...], h2.astype(BF16))
    prod_hi, prod_lo = split2(filters * feats)
    message = scale * (dotf(prod_hi, owner, NT) + dotf(prod_lo, owner, NT))
    sigm = 1.0 / (1.0 + jnp.exp(-message))
    out_slope = scale * eproj_ref[...] * (sigm * (1.0 + message * (1.0 - sigm)))
    os_hi, os_lo = split2(out_slope)
    slope_e = dotf(os_hi, owner) + dotf(os_lo, owner)
    fgrad = (slope_e * feats).astype(BF16)
    g2 = (dotf(w3_ref[...], fgrad) * slope2).astype(BF16)
    g1 = (dotf(w2_ref[...], g2) * slope1).astype(BF16)
    bg = dotf(w1_ref[...], g1)
    sgrad = -2.0 * jnp.sum(decay * basis * bg, 0, keepdims=True)
    pair_hi, pair_lo = split2(sgrad * sep)
    pairs = jnp.concatenate([pair_hi, pair_lo], 0)
    feat_part = dotf((filters * slope_e).astype(BF16), one, NT)
    pos_part = dotf(pairs, one, NT)
    own_part = dotf(pairs, owner, NT)
    return feat_part, pos_part[:8] + pos_part[8:], own_part[:8] + own_part[8:]


def layer_kernel(n, slots, m_here, coupling, inv_side, inv_total, sent_ref, mine_ref, data_ref, idx_ref, own_ref, pick_ref, proj_ref, w1_ref, w2_ref, w3_ref, eproj_ref, decay_ref, feat_ref, pos_ref, own_out_ref, w1t_ref, w2t_ref, w3t_ref, halo, table, gath, acc, ret_send, ret, sf, mh, res_send, res, halo_ss, halo_rs, gath_ss, gath_rs, ret_ss, ret_rs, res_ss, res_rs):
    me = lax.axis_index("dom")
    after, before = lax.rem(me + 1, n), lax.rem(me + n - 1, n)
    mesh_id = pl.DeviceIdType.MESH

    def loop(first, last, body):
        def step(t, carry):
            body(t)
            return carry

        lax.fori_loop(first, last, step, 0)

    def remote(src, dst, ss, rs, target):
        return pltpu.make_async_remote_copy(
            src_ref=src, dst_ref=dst, send_sem=ss, recv_sem=rs, device_id={"dom": target}, device_id_type=mesh_id
        )

    barrier = pltpu.get_barrier_semaphore()
    loop(1, n, lambda t: pl.semaphore_signal(barrier, inc=1, device_id={"dom": lax.rem(me + t, n)}, device_id_type=mesh_id))
    pl.semaphore_wait(barrier, n - 1)

    def halo_copy(k):
        return remote(sent_ref.at[k], halo.at[k], halo_ss.at[k], halo_rs.at[k], (after, before)[k])

    def ret_copy(k):
        return remote(ret_send, ret.at[k], ret_ss.at[k], ret_rs.at[k], (before, after)[k])

    def gath_copy(t):
        return remote(data_ref, gath.at[t], gath_ss.at[t], gath_rs.at[t], lax.rem(me + t, n))

    def res_copy(t):
        return remote(res_send.at[t], res.at[t], res_ss.at[t], res_rs.at[t], lax.rem(me + n - t, n))

    halo_copy(0).start()
    halo_copy(1).start()
    loop(1, n, lambda t: gath_copy(t).start())
    gath[0] = data_ref[...]

    here = mine_ref.shape[1]
    edges = idx_ref.shape[2]
    atoms = own_ref.shape[2]
    rows = table.shape[1]
    wide = w3t_ref.shape[0]
    chan = proj_ref.shape[1]
    weights = (w1t_ref, w1_ref, w2t_ref, w2_ref, w3t_ref, w3_ref, eproj_ref, decay_ref)
    first = lax.broadcasted_iota(jnp.int32, (atoms, edges), 0) * slots
    edge_id = lax.broadcasted_iota(jnp.int32, (atoms, edges), 1)
    owner = jnp.where((edge_id >= first) & (edge_id < first + slots), 1.0, 0.0).astype(BF16)
    table[:, :here] = mine_ref[...]
    acc[...] = jnp.zeros_like(acc)
    w1t_ref[...] = w1_ref[...].astype(F32).T.astype(BF16)
    w2t_ref[...] = w2_ref[...].astype(F32).T.astype(BF16)
    w3t_ref[...] = w3_ref[...].astype(F32).T.astype(BF16)
    halo_copy(0).wait()
    halo_copy(1).wait()
    table[:, here:] = halo[0] + halo[1]

    def edge_step(i):
        one = jnp.where(lax.broadcasted_iota(jnp.int32, (rows, edges), 0) == idx_ref[i], 1.0, 0.0).astype(BF16)
        feat_part, pos_part, own_part = edge_block(slots, idx_ref[i], own_ref[i], table[...], weights, one, owner)
        acc[0:wide, :] += feat_part
        acc[wide:, :] += pos_part
        own_out_ref[i] = own_part

    loop(0, idx_ref.shape[0], edge_step)
    ret_send[...] = acc[:, here:]
    ret_copy(0).start()
    ret_copy(1).start()

    loop(1, n, lambda t: gath_copy(t).wait())
    raw_sum = lax.fori_loop(0, n, lambda t, c: c + gath[t, 0:chan, :], jnp.zeros((chan, here), F32))
    mean = jnp.sum(raw_sum, 1, keepdims=True) * inv_total

    mp = mh.shape[1] // 2
    half = chan * MODES_Z

    def pair_numbers(shape, dim):
        local_p = lax.broadcasted_iota(jnp.int32, shape, dim)
        flat = me * m_here + local_p
        real = (local_p < m_here) & (flat < MODES_X * MODES_Y)
        return (flat // MODES_Y + 1).astype(F32), (flat % MODES_Y - MODES_Y // 2).astype(F32), real

    unit_x, unit_y = 2.0 * math.pi * inv_side, 2.0 * math.pi / CELL_SIDE
    k0, k1, _ = pair_numbers((mp, 1), 0)
    row0, row1, real = pair_numbers((half, mp), 1)
    row2 = (lax.broadcasted_iota(jnp.int32, (half, mp), 0) % MODES_Z - MODES_Z // 2).astype(F32)
    ksq = (row0 * unit_x) ** 2 + (row1 * unit_y) ** 2 + (row2 * unit_y) ** 2
    wt = jnp.where(real, 8.0 * coupling * jnp.exp(-ksq / 1024.0) / (ksq + 0.25), 0.0)
    k2 = lax.broadcasted_iota(jnp.int32, (MODES_Z, 1), 0).astype(F32) - float(MODES_Z // 2)

    def factors(t):
        q = gath[t, 0:chan, :] - mean
        xyz = gath[t, chan : chan + 8, :]
        x = xyz[0:1] * inv_side
        y = xyz[1:2] * (1.0 / CELL_SIDE)
        z = xyz[2:3] * (1.0 / CELL_SIDE)
        ec, es = sincos_turns(k0 * x + k1 * y)
        zc, zs = sincos_turns(k2 * z)
        a_re = (q[:, None, :] * zc[None, :, :]).reshape(half, here)
        a_im = (q[:, None, :] * zs[None, :, :]).reshape(half, here)
        return q, ec, es, zc, zs, [a_re, a_im]

    sf[...] = jnp.zeros_like(sf)

    def forward(t):
        q, ec, es, zc, zs, a = factors(t)
        sf[...] += dotb(jnp.concatenate(a + [zc, zs], 0), jnp.concatenate([ec, es], 0), NT)

    loop(0, n, forward)
    re = wt * (sf[:half, :mp] - sf[half : 2 * half, mp:])
    im = wt * (sf[:half, mp:] + sf[half : 2 * half, :mp])
    m1 = 2 * half + MODES_Z
    one_re = sf[2 * half : m1, :mp] - sf[m1:, mp:]
    one_im = sf[2 * half : m1, mp:] + sf[m1:, :mp]
    both = re.reshape(chan, MODES_Z, mp) * one_re[None] + im.reshape(chan, MODES_Z, mp) * one_im[None]
    grad_mean = jnp.sum(jnp.sum(both, 1), 1, keepdims=True) * inv_total
    m = jnp.concatenate([jnp.concatenate([re, im], 1), jnp.concatenate([im, -re], 1)], 0)
    mh[...] = m.astype(BF16)

    def backward(t):
        q, ec, es, zc, zs, a = factors(t)
        mm = mh[...]
        u = dotb(mm, jnp.concatenate([ec, es], 0), NN)
        ur = u[:half].reshape(chan, MODES_Z, here)
        ui = u[half:].reshape(chan, MODES_Z, here)
        cg = jnp.sum(zc[None] * ur + zs[None] * ui, 1) - grad_mean
        kz = k2 * (2.0 * math.pi / CELL_SIDE)
        lz = jnp.sum((kz * zc)[None] * ui - (kz * zs)[None] * ur, 1)
        lz = jnp.sum(q * lz, 0, keepdims=True)
        p = dotb(mm, jnp.concatenate(a, 0), TN)
        dp = ec * p[mp:] - es * p[:mp]
        lx = jnp.sum((k0 * unit_x) * dp, 0, keepdims=True)
        ly = jnp.sum((k1 * unit_y) * dp, 0, keepdims=True)
        return jnp.concatenate([cg, lx, ly, lz, jnp.zeros((5, here), F32)], 0)

    def send_back(t):
        res_send[t] = backward(t)
        res_copy(t).start()

    loop(1, n, send_back)
    res[0] = backward(0)
    ret_copy(0).wait()
    ret_copy(1).wait()
    back_hi, back_lo = split2(jnp.concatenate([ret[0], ret[1]], 1))
    back = dotf(back_hi, pick_ref[...], NT) + dotf(back_lo, pick_ref[...], NT)
    grads = acc[:, :here] + back
    loop(1, n, lambda t: res_copy(t).wait())
    total = lax.fori_loop(0, n, lambda t, c: c + res[t], jnp.zeros(res.shape[1:], F32))
    raw_hi, raw_lo = split2(total[:chan])
    feat = grads[:wide] + (dotf(proj_ref[...], raw_hi) + dotf(proj_ref[...], raw_lo))
    feat_ref[...] = feat.T.astype(BF16)
    own_sum = jnp.concatenate([own_out_ref[i] for i in range(idx_ref.shape[0])], 1)
    pos_ref[...] = (own_sum - (grads[wide:] + total[chan:]))[:3]


def local(places, nodes, partners, counts, exported, modes, proj, w1, w2, w3, eproj):
    n = lax.axis_size("dom")
    me = lax.axis_index("dom")
    here, wide = nodes.shape
    halo = exported.shape[0] // 2
    slots = partners.shape[1]
    side = float(n)
    total = n * here
    nrbf = w1.shape[0]
    chan = proj.shape[1]
    nodes_t = nodes.T

    pad8 = lambda a: jnp.pad(a, ((0, 5), (0, 0)))
    parts = jnp.concatenate([pad8(a) for a in split3(places)], 0)
    mine = jnp.concatenate([nodes_t, parts, jnp.zeros((8, here), BF16)], 0)
    order = jnp.concatenate([exported[halo:], exported[:halo]])
    lane = jnp.arange(4 * halo, dtype=jnp.int32)
    keep = (lane < halo) | (lane >= 3 * halo)
    target = jnp.where(keep, jnp.concatenate([order, order]), -1)
    pick = (jnp.arange(here, dtype=jnp.int32)[:, None] == target[None, :]).astype(BF16)
    step = jnp.where((lane < halo) & (me == n - 1), -side, 0.0) + jnp.where((lane >= 3 * halo) & (me == 0), side, 0.0)
    row = jnp.arange(wide + 32, dtype=jnp.int32)[:, None]
    sent = (dotf(mine, pick) + jnp.where(row == wide + 24, step[None, :], 0.0)).astype(BF16)
    sent = jnp.stack([sent[:, : 2 * halo], sent[:, 2 * halo :]])

    data = jnp.concatenate([dotf(proj.T, nodes_t), places, jnp.zeros((5, here), F32)], 0)
    pairs = MODES_X * MODES_Y
    m = -(-pairs // n)
    mp = -(-m // 8) * 8
    coupling = float(total * modes.shape[1]) ** (-0.5)
    half = chan * MODES_Z

    blk = math.gcd(here, 32)
    nblk = here // blk
    edges = blk * slots
    live = jnp.arange(slots, dtype=jnp.int32)[None, :] < counts[:, None]
    idx = jnp.where(live, partners, -1).reshape(nblk, 1, edges)
    own = parts.reshape(24, nblk, blk).transpose(1, 0, 2)
    decay = (0.02 * 64.0 ** (jnp.arange(nrbf, dtype=F32) / (nrbf - 1)))[:, None]
    args = [sent, mine, data, idx, own, pick, proj]
    args += [w1, w2, w3, eproj[:, None], decay]
    vmem = pl.BlockSpec(memory_space=pltpu.VMEM)
    dma = pltpu.SemaphoreType.DMA
    borrowed = 2 * halo
    feature_grad, forces = pl.pallas_call(
        functools.partial(layer_kernel, n, slots, m, coupling, 1.0 / side, 1.0 / total),
        out_shape=(
            jax.ShapeDtypeStruct((here, wide), BF16),
            jax.ShapeDtypeStruct((3, here), F32),
        ),
        in_specs=[vmem] * len(args),
        out_specs=(vmem,) * 2,
        scratch_shapes=[
            pltpu.VMEM((nblk, 8, blk), F32),
            pltpu.VMEM((w1.shape[1], nrbf), BF16),
            pltpu.VMEM(w2.shape, BF16),
            pltpu.VMEM(w3.shape, BF16),
            pltpu.VMEM((2, wide + 32, borrowed), BF16),
            pltpu.VMEM((wide + 32, here + borrowed), BF16),
            pltpu.VMEM((n, chan + 8, here), F32),
            pltpu.VMEM((wide + 8, here + borrowed), F32),
            pltpu.VMEM((wide + 8, borrowed), F32),
            pltpu.VMEM((2, wide + 8, borrowed), F32),
            pltpu.VMEM((2 * half + 2 * MODES_Z, 2 * mp), F32),
            pltpu.VMEM((2 * half, 2 * mp), BF16),
            pltpu.VMEM((n, chan + 8, here), F32),
            pltpu.VMEM((n, chan + 8, here), F32),
            dma((2,)), dma((2,)), dma((n,)), dma((n,)), dma((2,)), dma((2,)), dma((n,)), dma((n,)),
        ],
        compiler_params=pltpu.CompilerParams(collective_id=0, has_side_effects=True, vmem_limit_bytes=56 * 2**20),
        name="layer",
    )(*args)
    return (forces, feature_grad)


def solution(mesh):
    both = ("groups", "dom")
    in_specs = (P(None, both), P(both, None), P(both, None), P(both), P(both)) + (P(),) * 6
    out_specs = (P(None, both), P(both, None))
    return jax.shard_map(local, mesh=mesh, in_specs=in_specs, out_specs=out_specs, check_vma=False)
```

```python
import functools
import math

import jax
import jax.numpy as jnp
from jax import lax
from jax.experimental import pallas as pl
from jax.experimental.pallas import tpu as pltpu
from jax.sharding import PartitionSpec as P

CELL_SIDE = 4.0
PREC_HIGH = lax.Precision.HIGHEST
F32 = jnp.float32
BF16 = jnp.bfloat16
NT = (((1,), (1,)), ((), ()))
NN = (((1,), (0,)), ((), ()))
TN = (((0,), (0,)), ((), ()))
MODES_X = 48
MODES_Y = 16
MODES_Z = 16


def dotf(a, b, dims=NN):
    return lax.dot_general(a, b, dims, preferred_element_type=F32)


def split2(a):
    hi = a.astype(BF16)
    return hi, (a - hi.astype(F32)).astype(BF16)


def split3(a):
    hi = lax.reduce_precision(a, 8, 7)
    mid = lax.reduce_precision(a - hi, 8, 7)
    return hi.astype(BF16), mid.astype(BF16), (a - hi - mid).astype(BF16)


def dotb(a, b, dims):
    return dotf(a.astype(BF16), b.astype(BF16), dims)


def sincos_turns(turns):
    x = (turns - jnp.round(turns)) * (2.0 * math.pi)
    x2 = x * x
    c = jnp.full_like(x, 1.0 / math.factorial(16))
    for n in range(14, -1, -2):
        c = c * x2 + (-1.0) ** (n // 2) / math.factorial(n)
    s = jnp.full_like(x, 1.0 / math.factorial(17))
    for n in range(15, 0, -2):
        s = s * x2 + (-1.0) ** (n // 2) / math.factorial(n)
    return c, s * x


def edge_block(slots, idx, own_parts, table, weights, one, owner):
    w1t_ref, w1_ref, w2t_ref, w2_ref, w3t_ref, w3_ref, eproj_ref, decay_ref = weights
    scale = slots ** (-0.5)
    chan = w3t_ref.shape[0]
    got = dotf(table, one)
    feats = got[:chan]
    own = dotf(own_parts, owner)
    sep = got[chan : chan + 8] - own[0:8]
    for n in (8, 16):
        sep = sep + (got[chan + n : chan + n + 8] - own[n : n + 8])
    sep = sep + got[chan + 24 : chan + 32]
    sq = jnp.sum(sep * sep, 0, keepdims=True)
    decay = decay_ref[...]
    basis = jnp.exp(-decay * sq)
    pre1 = dotf(w1t_ref[...], basis.astype(BF16))
    sig1 = 0.5 * jnp.tanh(0.5 * pre1) + 0.5
    h1 = pre1 * sig1
    h1b, sig1b = h1.astype(BF16), sig1.astype(BF16)
    slope1 = sig1b + h1b * (1.0 - sig1b)
    pre2 = dotf(w2t_ref[...], h1b)
    sig2 = 0.5 * jnp.tanh(0.5 * pre2) + 0.5
    h2 = pre2 * sig2
    h2b, sig2b = h2.astype(BF16), sig2.astype(BF16)
    slope2 = sig2b + h2b * (1.0 - sig2b)
    filters = dotf(w3t_ref[...], h2b)
    message = scale * dotf((filters * feats).astype(BF16), owner, NT)
    sigm = 1.0 / (1.0 + jnp.exp(-message))
    out_slope = scale * eproj_ref[...] * (sigm * (1.0 + message * (1.0 - sigm)))
    os_hi, os_lo = split2(out_slope)
    slope_e = dotf(jnp.concatenate([os_hi, os_lo], 1), jnp.concatenate([owner, owner], 0))
    fgrad = (slope_e * feats).astype(BF16)
    g2 = dotf(w3_ref[...], fgrad).astype(BF16) * slope2
    g1 = dotf(w2_ref[...], g2).astype(BF16) * slope1
    bg = dotf(w1_ref[...], g1)
    sgrad = -2.0 * jnp.sum(decay * basis * bg, 0, keepdims=True)
    pair_hi, pair_lo = split2(sgrad * sep)
    pairs = jnp.concatenate([pair_hi, pair_lo], 0)
    feat_part = dotf((filters * slope_e).astype(BF16), one, NT)
    pos_part = dotf(pairs, one, NT)
    own_part = dotf(pairs, owner, NT)
    return feat_part, pos_part[:8] + pos_part[8:], own_part[:8] + own_part[8:]


def layer_kernel(n, slots, m_here, coupling, inv_side, inv_total, sent_ref, mine_ref, data_ref, idx_ref, own_ref, pick_ref, proj_ref, w1_ref, w2_ref, w3_ref, eproj_ref, decay_ref, feat_ref, pos_ref, own_out_ref, w1t_ref, w2t_ref, w3t_ref, halo, table, gath, acc, ret_send, ret, sf, mh, res_send, res, halo_ss, halo_rs, gath_ss, gath_rs, ret_ss, ret_rs, res_ss, res_rs):
    me = lax.axis_index("dom")
    after, before = lax.rem(me + 1, n), lax.rem(me + n - 1, n)
    mesh_id = pl.DeviceIdType.MESH

    def loop(first, last, body):
        def step(t, carry):
            body(t)
            return carry

        lax.fori_loop(first, last, step, 0)

    def remote(src, dst, ss, rs, target):
        return pltpu.make_async_remote_copy(
            src_ref=src, dst_ref=dst, send_sem=ss, recv_sem=rs, device_id={"dom": target}, device_id_type=mesh_id
        )

    barrier = pltpu.get_barrier_semaphore()
    loop(1, n, lambda t: pl.semaphore_signal(barrier, inc=1, device_id={"dom": lax.rem(me + t, n)}, device_id_type=mesh_id))
    pl.semaphore_wait(barrier, n - 1)

    def halo_copy(k):
        return remote(sent_ref.at[k], halo.at[k], halo_ss.at[k], halo_rs.at[k], (after, before)[k])

    def ret_copy(k):
        return remote(ret_send, ret.at[k], ret_ss.at[k], ret_rs.at[k], (before, after)[k])

    def gath_copy(t):
        return remote(data_ref, gath.at[t], gath_ss.at[t], gath_rs.at[t], lax.rem(me + t, n))

    def res_copy(t):
        return remote(res_send.at[t], res.at[t], res_ss.at[t], res_rs.at[t], lax.rem(me + n - t, n))

    halo_copy(0).start()
    halo_copy(1).start()
    loop(1, n, lambda t: gath_copy(t).start())
    gath[0] = data_ref[...]

    here = mine_ref.shape[1]
    edges = idx_ref.shape[2]
    atoms = own_ref.shape[2]
    rows = table.shape[1]
    wide = w3t_ref.shape[0]
    chan = proj_ref.shape[1]
    weights = (w1t_ref, w1_ref, w2t_ref, w2_ref, w3t_ref, w3_ref, eproj_ref, decay_ref)
    first = lax.broadcasted_iota(jnp.int32, (atoms, edges), 0) * slots
    edge_id = lax.broadcasted_iota(jnp.int32, (atoms, edges), 1)
    owner = jnp.where((edge_id >= first) & (edge_id < first + slots), 1.0, 0.0).astype(BF16)
    table[:, :here] = mine_ref[...]
    acc[...] = jnp.zeros_like(acc)
    w1t_ref[...] = w1_ref[...].astype(F32).T.astype(BF16)
    w2t_ref[...] = w2_ref[...].astype(F32).T.astype(BF16)
    w3t_ref[...] = w3_ref[...].astype(F32).T.astype(BF16)
    halo_copy(0).wait()
    halo_copy(1).wait()
    table[:, here:] = halo[0] + halo[1]

    def edge_step(i):
        one = jnp.where(lax.broadcasted_iota(jnp.int32, (rows, edges), 0) == idx_ref[i], 1.0, 0.0).astype(BF16)
        feat_part, pos_part, own_part = edge_block(slots, idx_ref[i], own_ref[i], table[...], weights, one, owner)
        acc[0:wide, :] += feat_part
        acc[wide:, :] += pos_part
        own_out_ref[i] = own_part

    loop(0, idx_ref.shape[0], edge_step)
    ret_send[...] = acc[:, here:]
    ret_copy(0).start()
    ret_copy(1).start()

    loop(1, n, lambda t: gath_copy(t).wait())
    raw_sum = lax.fori_loop(0, n, lambda t, c: c + gath[t, 0:chan, :], jnp.zeros((chan, here), F32))
    mean = jnp.sum(raw_sum, 1, keepdims=True) * inv_total

    mp = mh.shape[1] // 2
    half = chan * MODES_Z

    def pair_numbers(shape, dim):
        local_p = lax.broadcasted_iota(jnp.int32, shape, dim)
        flat = me * m_here + local_p
        real = (local_p < m_here) & (flat < MODES_X * MODES_Y)
        return (flat // MODES_Y + 1).astype(F32), (flat % MODES_Y - MODES_Y // 2).astype(F32), real

    unit_x, unit_y = 2.0 * math.pi * inv_side, 2.0 * math.pi / CELL_SIDE
    k0, k1, _ = pair_numbers((mp, 1), 0)
    row0, row1, real = pair_numbers((half, mp), 1)
    row2 = (lax.broadcasted_iota(jnp.int32, (half, mp), 0) % MODES_Z - MODES_Z // 2).astype(F32)
    ksq = (row0 * unit_x) ** 2 + (row1 * unit_y) ** 2 + (row2 * unit_y) ** 2
    wt = jnp.where(real, 8.0 * coupling * jnp.exp(-ksq / 1024.0) / (ksq + 0.25), 0.0)
    k2 = lax.broadcasted_iota(jnp.int32, (MODES_Z, 1), 0).astype(F32) - float(MODES_Z // 2)

    def factors(t):
        q = gath[t, 0:chan, :] - mean
        xyz = gath[t, chan : chan + 8, :]
        x = xyz[0:1] * inv_side
        y = xyz[1:2] * (1.0 / CELL_SIDE)
        z = xyz[2:3] * (1.0 / CELL_SIDE)
        ec, es = sincos_turns(k0 * x + k1 * y)
        zc, zs = sincos_turns(k2 * z)
        a_re = (q[:, None, :] * zc[None, :, :]).reshape(half, here)
        a_im = (q[:, None, :] * zs[None, :, :]).reshape(half, here)
        return q, ec, es, zc, zs, [a_re, a_im]

    sf[...] = jnp.zeros_like(sf)

    def forward(t):
        q, ec, es, zc, zs, a = factors(t)
        sf[...] += dotb(jnp.concatenate(a + [zc, zs], 0), jnp.concatenate([ec, es], 0), NT)

    loop(0, n, forward)
    re = wt * (sf[:half, :mp] - sf[half : 2 * half, mp:])
    im = wt * (sf[:half, mp:] + sf[half : 2 * half, :mp])
    m1 = 2 * half + MODES_Z
    one_re = sf[2 * half : m1, :mp] - sf[m1:, mp:]
    one_im = sf[2 * half : m1, mp:] + sf[m1:, :mp]
    both = re.reshape(chan, MODES_Z, mp) * one_re[None] + im.reshape(chan, MODES_Z, mp) * one_im[None]
    grad_mean = jnp.sum(jnp.sum(both, 1), 1, keepdims=True) * inv_total
    m = jnp.concatenate([jnp.concatenate([re, im], 1), jnp.concatenate([im, -re], 1)], 0)
    mh[...] = m.astype(BF16)

    def backward(t):
        q, ec, es, zc, zs, a = factors(t)
        mm = mh[...]
        u = dotb(mm, jnp.concatenate([ec, es], 0), NN)
        ur = u[:half].reshape(chan, MODES_Z, here)
        ui = u[half:].reshape(chan, MODES_Z, here)
        cg = jnp.sum(zc[None] * ur + zs[None] * ui, 1) - grad_mean
        kz = k2 * (2.0 * math.pi / CELL_SIDE)
        lz = jnp.sum((kz * zc)[None] * ui - (kz * zs)[None] * ur, 1)
        lz = jnp.sum(q * lz, 0, keepdims=True)
        p = dotb(mm, jnp.concatenate(a, 0), TN)
        dp = ec * p[mp:] - es * p[:mp]
        lx = jnp.sum((k0 * unit_x) * dp, 0, keepdims=True)
        ly = jnp.sum((k1 * unit_y) * dp, 0, keepdims=True)
        return jnp.concatenate([cg, lx, ly, lz, jnp.zeros((5, here), F32)], 0)

    def send_back(t):
        res_send[t] = backward(t)
        res_copy(t).start()

    loop(1, n, send_back)
    res[0] = backward(0)
    ret_copy(0).wait()
    ret_copy(1).wait()
    back_hi, back_lo = split2(jnp.concatenate([ret[0], ret[1]], 1))
    back = dotf(back_hi, pick_ref[...], NT) + dotf(back_lo, pick_ref[...], NT)
    grads = acc[:, :here] + back
    loop(1, n, lambda t: res_copy(t).wait())
    total = lax.fori_loop(0, n, lambda t, c: c + res[t], jnp.zeros(res.shape[1:], F32))
    raw_hi, raw_lo = split2(total[:chan])
    feat = grads[:wide] + (dotf(proj_ref[...], raw_hi) + dotf(proj_ref[...], raw_lo))
    feat_ref[...] = feat.T.astype(BF16)
    own_sum = jnp.concatenate([own_out_ref[i] for i in range(idx_ref.shape[0])], 1)
    pos_ref[...] = (own_sum - (grads[wide:] + total[chan:]))[:3]


def local(places, nodes, partners, counts, exported, modes, proj, w1, w2, w3, eproj):
    n = lax.axis_size("dom")
    me = lax.axis_index("dom")
    here, wide = nodes.shape
    halo = exported.shape[0] // 2
    slots = partners.shape[1]
    side = float(n)
    total = n * here
    nrbf = w1.shape[0]
    chan = proj.shape[1]
    nodes_t = nodes.T

    pad8 = lambda a: jnp.pad(a, ((0, 5), (0, 0)))
    parts = jnp.concatenate([pad8(a) for a in split3(places)], 0)
    mine = jnp.concatenate([nodes_t, parts, jnp.zeros((8, here), BF16)], 0)
    order = jnp.concatenate([exported[halo:], exported[:halo]])
    lane = jnp.arange(4 * halo, dtype=jnp.int32)
    keep = (lane < halo) | (lane >= 3 * halo)
    target = jnp.where(keep, jnp.concatenate([order, order]), -1)
    pick = (jnp.arange(here, dtype=jnp.int32)[:, None] == target[None, :]).astype(BF16)
    step = jnp.where((lane < halo) & (me == n - 1), -side, 0.0) + jnp.where((lane >= 3 * halo) & (me == 0), side, 0.0)
    row = jnp.arange(wide + 32, dtype=jnp.int32)[:, None]
    sent = (dotf(mine, pick) + jnp.where(row == wide + 24, step[None, :], 0.0)).astype(BF16)
    sent = jnp.stack([sent[:, : 2 * halo], sent[:, 2 * halo :]])

    data = jnp.concatenate([dotf(proj.T, nodes_t), places, jnp.zeros((5, here), F32)], 0)
    pairs = MODES_X * MODES_Y
    m = -(-pairs // n)
    mp = -(-m // 8) * 8
    coupling = float(total * modes.shape[1]) ** (-0.5)
    half = chan * MODES_Z

    blk = math.gcd(here, 32)
    nblk = here // blk
    edges = blk * slots
    live = jnp.arange(slots, dtype=jnp.int32)[None, :] < counts[:, None]
    idx = jnp.where(live, partners, -1).reshape(nblk, 1, edges)
    own = parts.reshape(24, nblk, blk).transpose(1, 0, 2)
    decay = (0.02 * 64.0 ** (jnp.arange(nrbf, dtype=F32) / (nrbf - 1)))[:, None]
    args = [sent, mine, data, idx, own, pick, proj]
    args += [w1, w2, w3, eproj[:, None], decay]
    vmem = pl.BlockSpec(memory_space=pltpu.VMEM)
    dma = pltpu.SemaphoreType.DMA
    borrowed = 2 * halo
    feature_grad, forces = pl.pallas_call(
        functools.partial(layer_kernel, n, slots, m, coupling, 1.0 / side, 1.0 / total),
        out_shape=(
            jax.ShapeDtypeStruct((here, wide), BF16),
            jax.ShapeDtypeStruct((3, here), F32),
        ),
        in_specs=[vmem] * len(args),
        out_specs=(vmem,) * 2,
        scratch_shapes=[
            pltpu.VMEM((nblk, 8, blk), F32),
            pltpu.VMEM((w1.shape[1], nrbf), BF16),
            pltpu.VMEM(w2.shape, BF16),
            pltpu.VMEM(w3.shape, BF16),
            pltpu.VMEM((2, wide + 32, borrowed), BF16),
            pltpu.VMEM((wide + 32, here + borrowed), BF16),
            pltpu.VMEM((n, chan + 8, here), F32),
            pltpu.VMEM((wide + 8, here + borrowed), F32),
            pltpu.VMEM((wide + 8, borrowed), F32),
            pltpu.VMEM((2, wide + 8, borrowed), F32),
            pltpu.VMEM((2 * half + 2 * MODES_Z, 2 * mp), F32),
            pltpu.VMEM((2 * half, 2 * mp), BF16),
            pltpu.VMEM((n, chan + 8, here), F32),
            pltpu.VMEM((n, chan + 8, here), F32),
            dma((2,)), dma((2,)), dma((n,)), dma((n,)), dma((2,)), dma((2,)), dma((n,)), dma((n,)),
        ],
        compiler_params=pltpu.CompilerParams(collective_id=0, has_side_effects=True, vmem_limit_bytes=56 * 2**20),
        name="layer",
    )(*args)
    return (forces, feature_grad)


def solution(mesh):
    both = ("groups", "dom")
    in_specs = (P(None, both), P(both, None), P(both, None), P(both), P(both)) + (P(),) * 6
    out_specs = (P(None, both), P(both, None))
    return jax.shard_map(local, mesh=mesh, in_specs=in_specs, out_specs=out_specs, check_vma=False)
```
